128 devices in a mesh: front: 4 (over x), helper: 32 (over z, y, core).
Axes of the slice: x: 4, y: 4, z: 4, core: 2. Of those that a mesh axis runs over, the one named last changes fastest.
Arguments:
- front: float32 [4, 8192, 8192], P('front', 'helper'), as said below
- tile_map: int32 [4, 52], P('front'), may hold values from 0 to 63, as said below
- live_tiles: int32 [4], P('front'), may hold values from 26 to 52, as said below
Outputs:
- factor: float32 [4, 8192, 1536], P('front', 'helper')
- pivots: float32 [4, 1536], P('front')
- parent: bfloat16 [4, 8192, 8192], P('front', 'helper')
The draws below stay inside these ranges and needn't reach their ends.
Inputs may be any that keep to these rules, and one draw needn't show every extreme that they name: `tile_map`: the 52 entries of one front are distinct. `live_tiles`: some front has all 52 tiles live. Each front is symmetric and positive definite.
All inputs are finite; a program needn't handle non-finite values.
Results may differ from the reference program's by a relative error of at most 0.0021.
Values may be sent and summed in bfloat16 or wider, within the bound.
No kernel may reach another device: no remote copies, remote signals or barrier semaphores. Data moves between devices by JAX's collectives and lax.ppermute only.
A program may use at most 192 MiB of HBM per device.

```python
import jax
import jax.numpy as jnp
from jax import lax

F = 8192
PB = 512
NPB = 3
TILE = 128
NPIV = 1536
CT = 52
PT = 64
N_FRONT = 4


def gram_of(basis_rows):
    product_matrix = jnp.dot(basis_rows, basis_rows.T, precision=lax.Precision.HIGHEST) / basis_rows.shape[1]
    return (product_matrix + product_matrix.T) * 0.5


def draw_front(key, part):
    key = jax.random.fold_in(key, 11)
    key_basis, key_shift = jax.random.split(key, 2)
    rank_count = F // 2
    basis_rows = jnp.clip(jax.random.normal(key_basis, (N_FRONT, F, rank_count), jnp.float32), -4.0, 4.0)
    diag_shift = jax.random.uniform(key_shift, (N_FRONT, F), jnp.float32, 0.4, 0.8)
    gram_blocks = lax.map(gram_of, basis_rows)
    on_diag = lax.iota(jnp.int32, F)[:, None] == lax.iota(jnp.int32, F)[None, :]
    return gram_blocks + jnp.where(on_diag[None], diag_shift[:, :, None], jnp.float32(0.0))


def draw_tile_map(key, part):
    key = jax.random.fold_in(key, 12)
    keys = jax.random.split(key, N_FRONT)
    orders = jax.vmap(lambda one_key: jax.random.permutation(one_key, PT))(keys)
    return orders[:, :CT].astype(jnp.int32)


def draw_live_tiles(key, part):
    key = jax.random.fold_in(key, 13)
    key_count, key_full = jax.random.split(key)
    counts = jax.random.randint(key_count, (N_FRONT,), CT // 2, CT + 1)
    full_group = jax.random.randint(key_full, (), 0, N_FRONT)
    return jnp.where(lax.iota(jnp.int32, N_FRONT) == full_group, CT, counts).astype(jnp.int32)


def setup_inputs(seed: int = 0) -> dict:
    seeds = jax.random.split(jax.random.key(seed), 4)
    front = draw_front(jax.random.fold_in(seeds[3], 71), 0)
    tile_map = draw_tile_map(jax.random.fold_in(seeds[3], 71), 0)
    live_tiles = draw_live_tiles(jax.random.fold_in(seeds[3], 71), 0)
    return dict(front=front, tile_map=tile_map, live_tiles=live_tiles)


def partial_factor(matrix):
    ordering_length = matrix.shape[0]
    row_ids = lax.iota(jnp.int32, ordering_length)
    columns = []
    pivot_list = []
    for block_index in range(NPB):
        lower_bound = block_index * PB
        high_edge = lower_bound + PB
        chol_block = jnp.linalg.cholesky(matrix[lower_bound:high_edge, lower_bound:high_edge])
        panel = matrix[:, lower_bound:high_edge]
        scaled = jax.scipy.linalg.solve_triangular(chol_block, panel.T, lower=True).T
        scaled = jnp.where((row_ids >= lower_bound)[:, None], scaled, jnp.float32(0.0))
        diag_values = jnp.diagonal(chol_block)
        columns.append(scaled / diag_values[None, :])
        pivot_list.append(diag_values * diag_values)
        rounded = lax.optimization_barrier(scaled.astype(jnp.bfloat16)).astype(jnp.float32)
        schur_update = jnp.dot(rounded, rounded[high_edge:].T, precision=lax.Precision.HIGHEST)
        matrix = matrix.at[:, high_edge:].add(-schur_update)
    return (matrix, jnp.concatenate(columns, axis=1), jnp.concatenate(pivot_list))

def extend_place(matrix, mapping, live_count):
    contrib = matrix[NPIV:, NPIV:].astype(jnp.bfloat16)
    tile_ids = lax.iota(jnp.int32, CT)
    target = jnp.where(tile_ids < live_count, mapping, PT).astype(jnp.int32)
    source = jnp.full((PT + 1,), CT, jnp.int32).at[target].set(tile_ids)[:PT]
    block_entries = contrib.reshape(CT, TILE, CT, TILE)
    block_entries = jnp.pad(block_entries, ((0, 1), (0, 0), (0, 1), (0, 0)))
    picked = block_entries[source][:, :, source]
    return picked.transpose(2, 3, 0, 1).reshape(PT * TILE, PT * TILE)

def reference(front, tile_map, live_tiles):
    factor_list = []
    pivot_rows = []
    positioned_rows = []
    for group in range(front.shape[0]):
        matrix, factor_cols, pivot_values = partial_factor(front[group])
        factor_list.append(factor_cols)
        pivot_rows.append(pivot_values)
        positioned_rows.append(extend_place(matrix, tile_map[group], live_tiles[group]))
    positioned = jnp.stack(positioned_rows)
    parent = jnp.roll(positioned, 1, axis=0)
    return (jnp.stack(factor_list), jnp.stack(pivot_rows), parent)
```

```python
import functools

import jax
import jax.numpy as jnp
from jax import lax
from jax.experimental import pallas as pl
from jax.experimental.pallas import tpu as pltpu
from jax.sharding import PartitionSpec as P

PB = 512
NPB = 3
TILE = 128
NPIV = 1536
CT = 52
PT = 64
SKIP = NPIV // TILE
VMEM_LIMIT = 48 << 20
HIGHEST = lax.Precision.HIGHEST


def shifted(array, axis, by):
    count = lax.axis_size(axis)
    return lax.ppermute(array, axis, [(i, (i + by) % count) for i in range(count)])


def dot_nt(a, b, precision=None):
    return lax.dot_general(
        a, b, (((1,), (1,)), ((), ())), precision=precision, preferred_element_type=jnp.float32
    )


def dot_nn(a, b, precision=None):
    return lax.dot_general(
        a, b, (((1,), (0,)), ((), ())), precision=precision, preferred_element_type=jnp.float32
    )


def leaf_inverse(strips):
    lanes = lax.broadcasted_iota(jnp.int32, (8, TILE), 1)
    subs = lax.broadcasted_iota(jnp.int32, (8, TILE), 0)
    count = len(strips)
    t = list(strips)
    e = [jnp.where(lanes == subs + 8 * r, 1.0, 0.0).astype(jnp.float32) for r in range(count)]
    diag = jnp.zeros((8, TILE), jnp.float32)

    def row_splat(v, i):
        return jnp.broadcast_to(v[i : i + 1, :], (8, TILE))

    def lane_splat(v, c):
        return jnp.broadcast_to(v[:, c : c + 1], (8, TILE))

    out = []
    for s in range(count):
        k = 8 * s
        last = s + 1 == count
        b = [lane_splat(t[s], k + j) for j in range(8)]
        corner = [[row_splat(b[j], i) for j in range(i + 1)] for i in range(8)]
        rt = None if last else [row_splat(t[s], i) for i in range(8)]
        re = [row_splat(e[s], i) for i in range(8)]
        l = [[None] * 8 for _ in range(8)]
        inv = []
        for j in range(8):
            iv = lax.rsqrt(corner[j][j])
            inv.append(iv)
            diag = jnp.where(lanes == k + j, corner[j][j] * iv, diag)
            for i in range(j + 1, 8):
                l[i][j] = corner[i][j] * iv
            for i in range(j + 1, 8):
                for m in range(j + 1, i + 1):
                    corner[i][m] = corner[i][m] - l[i][j] * l[m][j]
            re[j] = re[j] * iv
            if not last:
                rt[j] = rt[j] * iv
            for i in range(j + 1, 8):
                re[i] = re[i] - l[i][j] * re[j]
                if not last:
                    rt[i] = rt[i] - l[i][j] * rt[j]
        rows = re[0]
        for i in range(1, 8):
            rows = jnp.where(subs == i, re[i], rows)
        out.append(rows)
        for r in range(s + 1, count):
            c = [lane_splat(t[r], k + j) for j in range(8)]
            for j in range(8):
                c[j] = c[j] * inv[j]
                for m in range(j + 1, 8):
                    c[m] = c[m] - c[j] * l[m][j]
                t[r] = t[r] - c[j] * rt[j]
                e[r] = e[r] - c[j] * re[j]
    return out, diag[0:1, :]


def block_inverse(a_ref, x_ref, diag_ref, leaf_ref):
    steps = PB // TILE
    x_ref[...] = jnp.zeros_like(x_ref)

    def step(j, carry):
        o = pl.multiple_of(j * TILE, TILE)
        strips = [
            a_ref[pl.ds(pl.multiple_of(o + 8 * r, 8), 8), pl.ds(o, TILE)] for r in range(TILE // 8)
        ]
        rows, diag = leaf_inverse(strips)
        for r in range(TILE // 8):
            leaf_ref[8 * r : 8 * r + 8, :] = rows[r]
        diag_ref[:, pl.ds(o, TILE)] = diag
        for q in range(steps):

            @pl.when(j == q)
            def _():
                lo, hi = q * TILE, (q + 1) * TILE
                leaf = leaf_ref[...]
                x_ref[lo:hi, lo:hi] = leaf
                if q:
                    x_ref[lo:hi, 0:lo] = dot_nn(leaf, x_ref[lo:hi, 0:lo], HIGHEST)
                if q + 1 < steps:
                    p = dot_nt(a_ref[hi:PB, lo:hi], leaf, HIGHEST)
                    for b in range(q + 1, steps):
                        pb = p[(b - q - 1) * TILE :]
                        a_ref[b * TILE : PB, b * TILE : (b + 1) * TILE] -= dot_nt(pb, pb[0:TILE], HIGHEST)
                    x_ref[hi:PB, 0:hi] -= dot_nn(p, x_ref[lo:hi, 0:hi], HIGHEST)

        return carry

    lax.fori_loop(0, steps, step, 0)


def finish_panel(k, first_row, panel, inv, diag, factor_ref, wb_ref):
    w = dot_nt(panel, inv, HIGHEST)
    rows = lax.broadcasted_iota(jnp.int32, w.shape, 0) + first_row
    w = jnp.where(rows >= k * PB, w, 0.0)
    factor_ref[...] = w * (1.0 / diag)
    wb_ref[...] = w.astype(jnp.bfloat16)


def lead(ref):
    return ref[...].reshape(PB, PB)


def kernel_0(row_ref, a00, panel, inv_ref, diag_ref, factor_ref, wb_ref, a_ref, leaf_ref):
    for s in range(2):
        a_ref[s * 256 : (s + 1) * 256, :] = a00[:, s].reshape(256, PB)
    block_inverse(a_ref, inv_ref, diag_ref, leaf_ref)
    finish_panel(0, row_ref[0], panel[0], inv_ref[...], diag_ref[...], factor_ref, wb_ref)


def put_block(ref):
    return jnp.concatenate([ref[:, s].reshape(256, PB) for s in range(2)], axis=0)


def kernel_1(
    row_ref, a10, a11, panel, inv0, wb0, factor_in, inv_ref, diag_ref, factor_ref, wb_ref, lb10_ref, a_ref, leaf_ref
):
    lb10 = dot_nt(put_block(a10), inv0[...], HIGHEST).astype(jnp.bfloat16)
    lb10_ref[...] = lb10
    a_ref[...] = put_block(a11) - dot_nt(lb10, lb10)
    block_inverse(a_ref, inv_ref, diag_ref, leaf_ref)
    mine = panel[0] - dot_nt(wb0[...], lb10_ref[...])
    finish_panel(1, row_ref[0], mine, inv_ref[...], diag_ref[...], factor_ref, wb_ref)


def kernel_2(
    row_ref, a20, a21, a22, panel, inv0, inv1, lb10, wb0, wb1, factor_in, diag_ref, factor_ref, wb_ref, a_ref, leaf_ref,
    inv_ref, lb20_ref, lb21_ref
):
    lb20 = dot_nt(put_block(a20), inv0[...], HIGHEST).astype(jnp.bfloat16)
    lb20_ref[...] = lb20
    lb21 = dot_nt(put_block(a21) - dot_nt(lb20, lb10[...]), inv1[...], HIGHEST).astype(jnp.bfloat16)
    lb21_ref[...] = lb21
    a_ref[...] = put_block(a22) - dot_nt(lb20, lb20) - dot_nt(lb21, lb21)
    block_inverse(a_ref, inv_ref, diag_ref, leaf_ref)
    mine = panel[0] - dot_nt(wb0[...], lb20_ref[...]) - dot_nt(wb1[...], lb21_ref[...])
    finish_panel(2, row_ref[0], mine, inv_ref[...], diag_ref[...], factor_ref, wb_ref)


def whole(shape):
    return pl.BlockSpec(shape, lambda i: (0,) * len(shape))


def factor_step(k, first_row, front, leading, carried, factor):
    rows = front.shape[1]
    specs = [pl.BlockSpec(memory_space=pltpu.SMEM)]
    args = [first_row]
    for array, i, j in leading:
        specs.append(pl.BlockSpec((array.shape[0], 2, 8, PB), lambda _, i=i, j=j: (0, i, 0, j)))
        args.append(array)
    specs.append(pl.BlockSpec((1, rows, PB), lambda _: (0, 0, k)))
    args.append(front)
    for array in carried:
        specs.append(whole(array.shape))
        args.append(array)
    square = jax.ShapeDtypeStruct((PB, PB), jnp.float32)
    diag = jax.ShapeDtypeStruct((1, PB), jnp.float32)
    factors = jax.ShapeDtypeStruct((rows, NPIV), jnp.float32)
    wb = jax.ShapeDtypeStruct((rows, PB), jnp.bfloat16)
    factor_spec = pl.BlockSpec((rows, PB), lambda _: (0, k))
    outs = [diag, factors, wb]
    out_specs = [whole(diag.shape), factor_spec, whole(wb.shape)]
    scratch = [pltpu.VMEM((PB, PB), jnp.float32), pltpu.VMEM((TILE, TILE), jnp.float32)]
    if k < 2:
        outs.insert(0, square)
        out_specs.insert(0, whole(square.shape))
    else:
        scratch += [pltpu.VMEM((PB, PB), jnp.float32)] + [pltpu.VMEM((PB, PB), jnp.bfloat16)] * 2
    if k == 1:
        outs.append(jax.ShapeDtypeStruct((PB, PB), jnp.bfloat16))
        out_specs.append(whole((PB, PB)))
    aliases = {}
    if k:
        specs.append(pl.BlockSpec(memory_space=pl.ANY))
        args.append(factor)
        aliases = {len(args) - 1: 1 if k == 1 else 1}
        if k == 1:
            aliases = {len(args) - 1: 2}
    return pl.pallas_call(
        (kernel_0, kernel_1, kernel_2)[k],
        grid=(1,),
        in_specs=specs,
        out_specs=out_specs,
        out_shape=outs,
        scratch_shapes=scratch,
        input_output_aliases=aliases,
        compiler_params=pltpu.CompilerParams(vmem_limit_bytes=VMEM_LIMIT),
        cost_estimate=pl.CostEstimate(flops=20_000_000_000, bytes_accessed=4_000_000, transcendentals=0),
        name=f"pivot_block_{k}",
    )(*args)


def place_kernel(tiles_ref, info_ref, t0, t1, w0, w1, own, out_ref):
    i = pl.program_id(0)
    rows = own.shape[0]
    row_tile = (lax.broadcasted_iota(jnp.int32, (rows, TILE), 0) + info_ref[0] - NPIV) // TILE
    row_ids = lax.broadcasted_iota(jnp.int32, (rows, TILE), 0) + info_ref[0]
    row_live = (row_ids >= NPIV) & (row_tile < info_ref[1])
    for half, (t, w) in enumerate(((t0, w0), (t1, w1))):
        live = tiles_ref[2 * i + half] < CT
        value = t[...] - dot_nt(own[...], w[...])
        out_ref[0, :, half * TILE : (half + 1) * TILE] = jnp.where(row_live & live, value, 0.0).astype(jnp.bfloat16)


def place(tiles, info, base, own, gathered, helpers):
    rows, depth = own.shape

    def pick(half):
        return lambda i, tiles, info: (0, jnp.minimum(tiles[2 * i + half], CT - 1))

    def pick_rows(half):
        return lambda i, tiles, info: (SKIP + jnp.minimum(tiles[2 * i + half], CT - 1), 0)

    return pl.pallas_call(
        place_kernel,
        grid_spec=pltpu.PrefetchScalarGridSpec(
            num_scalar_prefetch=2,
            grid=(helpers,),
            in_specs=[
                pl.BlockSpec((rows, TILE), pick(0)),
                pl.BlockSpec((rows, TILE), pick(1)),
                pl.BlockSpec((TILE, depth), pick_rows(0)),
                pl.BlockSpec((TILE, depth), pick_rows(1)),
                pl.BlockSpec((rows, depth), lambda i, tiles, info: (0, 0)),
            ],
            out_specs=pl.BlockSpec((1, rows, 2 * TILE), lambda i, tiles, info: (i, 0, 0)),
        ),
        out_shape=jax.ShapeDtypeStruct((helpers, rows, 2 * TILE), jnp.bfloat16),
        compiler_params=pltpu.CompilerParams(vmem_limit_bytes=VMEM_LIMIT),
        name="contribution_tiles",
    )(tiles, info, base, base, gathered, gathered, own)


def assemble_kernel(tiles_ref, *refs):
    out_ref = refs[-1]
    i = pl.program_id(0)
    count = len(refs) - 1
    for half in range(count):
        live = tiles_ref[count * i + half] < CT
        value = refs[half][...].astype(jnp.float32).T
        out_ref[:, half * TILE : (half + 1) * TILE] = jnp.where(live, value, 0.0).astype(jnp.bfloat16)


def assemble(tiles, incoming, per_step=4):
    total, rows = incoming.shape

    def pick_rows(half):
        return lambda i, tiles: (SKIP + jnp.minimum(tiles[per_step * i + half], CT - 1), 0)

    return pl.pallas_call(
        assemble_kernel,
        grid_spec=pltpu.PrefetchScalarGridSpec(
            num_scalar_prefetch=1,
            grid=(PT // per_step,),
            in_specs=[pl.BlockSpec((TILE, rows), pick_rows(h)) for h in range(per_step)],
            out_specs=pl.BlockSpec((rows, per_step * TILE), lambda i, tiles: (0, i)),
        ),
        out_shape=jax.ShapeDtypeStruct((rows, total), jnp.bfloat16),
        compiler_params=pltpu.CompilerParams(vmem_limit_bytes=VMEM_LIMIT),
        name="parent_rows",
    )(tiles, *([incoming] * per_step))


def exchange(array):
    return lax.all_to_all(array, "helper", split_axis=0, concat_axis=0, tiled=True)


def local(front, tile_map, live_tiles):
    _, rows, order = front.shape
    helpers = lax.axis_size("helper")
    helper = lax.axis_index("helper")
    first_row = (helper * rows).astype(jnp.int32).reshape(1)
    piece = rows // helpers

    panel = front[0, :, :NPIV]
    scattered = exchange(panel.reshape(helpers, piece, NPIV))[: NPIV // rows]
    block_0 = exchange(
        jnp.broadcast_to(scattered[None, :2, :, :PB], (helpers, 2, piece, PB))
    )
    rest = lax.all_gather(scattered[2:], "helper", axis=0)

    moved = shifted(front[0, :, NPIV:], "front", 1)
    tiling = shifted(jnp.concatenate([tile_map[0], live_tiles]), "front", 1)
    mapping, live_count = tiling[:CT], tiling[CT]
    tile_ids = lax.iota(jnp.int32, CT)
    match = (mapping[None, :] == lax.iota(jnp.int32, PT)[:, None]) & (tile_ids[None, :] < live_count)
    tiles = jnp.where(jnp.any(match, axis=1), jnp.sum(jnp.where(match, tile_ids[None, :], 0), axis=1), CT)
    tiles = tiles.astype(jnp.int32)
    info = jnp.concatenate([first_row, live_count.reshape(1)])

    inv0, diag0, factor, wb0 = factor_step(0, first_row, front, [(block_0, 0, 0)], [], None)
    own0 = shifted(wb0, "front", 1)
    all0 = lax.all_gather(own0, "helper", axis=0, tiled=True)
    inv1, diag1, factor, wb1, lb10 = factor_step(
        1, first_row, front, [(rest, 0, 0), (rest, 0, 1)], [inv0, wb0], factor
    )
    diag2, factor, wb2 = factor_step(
        2, first_row, front, [(rest, 1, 0), (rest, 1, 1), (rest, 1, 2)], [inv0, inv1, lb10, wb0, wb1], factor
    )
    own12 = shifted(jnp.concatenate([wb1, wb2], axis=1), "front", 1)
    all12 = lax.all_gather(own12, "helper", axis=0, tiled=True)

    base = moved - dot_nt(own0, all0[NPIV:])
    outgoing = place(tiles, info, base, own12, all12, helpers)
    incoming = exchange(outgoing).reshape(order, rows)
    parent = assemble(tiles, incoming)
    diag = jnp.concatenate([diag0, diag1, diag2], axis=1)
    return factor[None], diag * diag, parent[None]


def solution(mesh):
    placed = (P("front", "helper", None), P("front", None), P("front"))
    return jax.shard_map(
        local,
        mesh=mesh,
        in_specs=placed,
        out_specs=(P("front", "helper", None), P("front", None), P("front", "helper", None)),
        check_vma=False,
    )
```

```python
import functools

import jax
import jax.numpy as jnp
from jax import lax
from jax.experimental import pallas as pl
from jax.experimental.pallas import tpu as pltpu
from jax.sharding import PartitionSpec as P

PB = 512
NPB = 3
TILE = 128
NPIV = 1536
CT = 52
PT = 64
SKIP = NPIV // TILE
VMEM_LIMIT = 48 << 20
CHUNKS = (32, 32, 40, 48, 104)
HIGHEST = lax.Precision.HIGHEST


def shifted(array, axis, by):
    count = lax.axis_size(axis)
    return lax.ppermute(array, axis, [(i, (i + by) % count) for i in range(count)])


def dot_nt(a, b, precision=None):
    return lax.dot_general(
        a, b, (((1,), (1,)), ((), ())), precision=precision, preferred_element_type=jnp.float32
    )


def dot_nn(a, b, precision=None):
    return lax.dot_general(
        a, b, (((1,), (0,)), ((), ())), precision=precision, preferred_element_type=jnp.float32
    )


def leaf_inverse(strips):
    lanes = lax.broadcasted_iota(jnp.int32, (8, TILE), 1)
    subs = lax.broadcasted_iota(jnp.int32, (8, TILE), 0)
    count = len(strips)
    t = list(strips)
    e = [jnp.where(lanes == subs + 8 * r, 1.0, 0.0).astype(jnp.float32) for r in range(count)]
    diag = jnp.zeros((8, TILE), jnp.float32)

    def row_splat(v, i):
        return jnp.broadcast_to(v[i : i + 1, :], (8, TILE))

    def lane_splat(v, c):
        return jnp.broadcast_to(v[:, c : c + 1], (8, TILE))

    out = []
    for s in range(count):
        k = 8 * s
        last = s + 1 == count
        b = [lane_splat(t[s], k + j) for j in range(8)]
        corner = [[row_splat(b[j], i) for j in range(i + 1)] for i in range(8)]
        rt = None if last else [row_splat(t[s], i) for i in range(8)]
        re = [row_splat(e[s], i) for i in range(8)]
        l = [[None] * 8 for _ in range(8)]
        inv = []
        for j in range(8):
            iv = lax.rsqrt(corner[j][j])
            inv.append(iv)
            diag = jnp.where(lanes == k + j, corner[j][j] * iv, diag)
            for i in range(j + 1, 8):
                l[i][j] = corner[i][j] * iv
            for i in range(j + 1, 8):
                for m in range(j + 1, i + 1):
                    corner[i][m] = corner[i][m] - l[i][j] * l[m][j]
            re[j] = re[j] * iv
            if not last:
                rt[j] = rt[j] * iv
            for i in range(j + 1, 8):
                re[i] = re[i] - l[i][j] * re[j]
                if not last:
                    rt[i] = rt[i] - l[i][j] * rt[j]
        rows = re[0]
        for i in range(1, 8):
            rows = jnp.where(subs == i, re[i], rows)
        out.append(rows)
        for r in range(s + 1, count):
            c = [lane_splat(t[r], k + j) for j in range(8)]
            for j in range(8):
                c[j] = c[j] * inv[j]
                for m in range(j + 1, 8):
                    c[m] = c[m] - c[j] * l[m][j]
                t[r] = t[r] - c[j] * rt[j]
                e[r] = e[r] - c[j] * re[j]
    return out, diag[0:1, :]


def block_inverse(a_ref, x_ref, diag_ref, leaf_ref):
    steps = PB // TILE
    x_ref[...] = jnp.zeros_like(x_ref)

    def step(j, carry):
        o = pl.multiple_of(j * TILE, TILE)
        strips = [
            a_ref[pl.ds(pl.multiple_of(o + 8 * r, 8), 8), pl.ds(o, TILE)] for r in range(TILE // 8)
        ]
        rows, diag = leaf_inverse(strips)
        for r in range(TILE // 8):
            leaf_ref[8 * r : 8 * r + 8, :] = rows[r]
        diag_ref[:, pl.ds(o, TILE)] = diag
        for q in range(steps):

            @pl.when(j == q)
            def _():
                lo, hi = q * TILE, (q + 1) * TILE
                leaf = leaf_ref[...]
                x_ref[lo:hi, lo:hi] = leaf
                if q:
                    x_ref[lo:hi, 0:lo] = dot_nn(leaf, x_ref[lo:hi, 0:lo], HIGHEST)
                if q + 1 < steps:
                    p = dot_nt(a_ref[hi:PB, lo:hi], leaf, HIGHEST)
                    for b in range(q + 1, steps):
                        pb = p[(b - q - 1) * TILE :]
                        a_ref[b * TILE : PB, b * TILE : (b + 1) * TILE] -= dot_nt(pb, pb[0:TILE], HIGHEST)
                    x_ref[hi:PB, 0:hi] -= dot_nn(p, x_ref[lo:hi, 0:hi], HIGHEST)

        return carry

    lax.fori_loop(0, steps, step, 0)


def finish_panel(k, first_row, panel, inv, diag, factor_ref, wb_ref):
    w = dot_nt(panel, inv, HIGHEST)
    rows = lax.broadcasted_iota(jnp.int32, w.shape, 0) + first_row
    w = jnp.where(rows >= k * PB, w, 0.0)
    factor_ref[...] = w * (1.0 / diag)
    wb_ref[...] = w.astype(jnp.bfloat16)


def lead(ref):
    return ref[...].reshape(PB, PB)


def kernel_0(row_ref, a00, panel, inv_ref, diag_ref, factor_ref, wb_ref, a_ref, leaf_ref):
    for s in range(2):
        a_ref[s * 256 : (s + 1) * 256, :] = a00[:, s].reshape(256, PB)
    block_inverse(a_ref, inv_ref, diag_ref, leaf_ref)
    finish_panel(0, row_ref[0], panel[0], inv_ref[...], diag_ref[...], factor_ref, wb_ref)


def put_block(ref):
    return jnp.concatenate([ref[:, s].reshape(256, PB) for s in range(2)], axis=0)


def kernel_1(
    row_ref, a10, a11, panel, inv0, wb0, factor_in, inv_ref, diag_ref, factor_ref, wb_ref, lb10_ref, a_ref, leaf_ref
):
    lb10 = dot_nt(put_block(a10), inv0[...], HIGHEST).astype(jnp.bfloat16)
    lb10_ref[...] = lb10
    a_ref[...] = put_block(a11) - dot_nt(lb10, lb10)
    block_inverse(a_ref, inv_ref, diag_ref, leaf_ref)
    mine = panel[0] - dot_nt(wb0[...], lb10_ref[...])
    finish_panel(1, row_ref[0], mine, inv_ref[...], diag_ref[...], factor_ref, wb_ref)


def kernel_2(
    row_ref, a20, a21, a22, panel, inv0, inv1, lb10, wb0, wb1, factor_in, diag_ref, factor_ref, wb_ref, a_ref, leaf_ref,
    inv_ref, lb20_ref, lb21_ref
):
    lb20 = dot_nt(put_block(a20), inv0[...], HIGHEST).astype(jnp.bfloat16)
    lb20_ref[...] = lb20
    lb21 = dot_nt(put_block(a21) - dot_nt(lb20, lb10[...]), inv1[...], HIGHEST).astype(jnp.bfloat16)
    lb21_ref[...] = lb21
    a_ref[...] = put_block(a22) - dot_nt(lb20, lb20) - dot_nt(lb21, lb21)
    block_inverse(a_ref, inv_ref, diag_ref, leaf_ref)
    mine = panel[0] - dot_nt(wb0[...], lb20_ref[...]) - dot_nt(wb1[...], lb21_ref[...])
    finish_panel(2, row_ref[0], mine, inv_ref[...], diag_ref[...], factor_ref, wb_ref)


def whole(shape):
    return pl.BlockSpec(shape, lambda i: (0,) * len(shape))


def factor_step(k, first_row, front, leading, carried, factor):
    rows = front.shape[1]
    specs = [pl.BlockSpec(memory_space=pltpu.SMEM)]
    args = [first_row]
    for array, i, j in leading:
        specs.append(pl.BlockSpec((array.shape[0], 2, 8, PB), lambda _, i=i, j=j: (0, i, 0, j)))
        args.append(array)
    specs.append(pl.BlockSpec((1, rows, PB), lambda _: (0, 0, k)))
    args.append(front)
    for array in carried:
        specs.append(whole(array.shape))
        args.append(array)
    square = jax.ShapeDtypeStruct((PB, PB), jnp.float32)
    diag = jax.ShapeDtypeStruct((1, PB), jnp.float32)
    factors = jax.ShapeDtypeStruct((rows, NPIV), jnp.float32)
    wb = jax.ShapeDtypeStruct((rows, PB), jnp.bfloat16)
    factor_spec = pl.BlockSpec((rows, PB), lambda _: (0, k))
    outs = [diag, factors, wb]
    out_specs = [whole(diag.shape), factor_spec, whole(wb.shape)]
    scratch = [pltpu.VMEM((PB, PB), jnp.float32), pltpu.VMEM((TILE, TILE), jnp.float32)]
    if k < 2:
        outs.insert(0, square)
        out_specs.insert(0, whole(square.shape))
    else:
        scratch += [pltpu.VMEM((PB, PB), jnp.float32)] + [pltpu.VMEM((PB, PB), jnp.bfloat16)] * 2
    if k == 1:
        outs.append(jax.ShapeDtypeStruct((PB, PB), jnp.bfloat16))
        out_specs.append(whole((PB, PB)))
    aliases = {}
    if k:
        specs.append(pl.BlockSpec(memory_space=pl.ANY))
        args.append(factor)
        aliases = {len(args) - 1: 2 if k == 1 else 1}
    return pl.pallas_call(
        (kernel_0, kernel_1, kernel_2)[k],
        grid=(1,),
        in_specs=specs,
        out_specs=out_specs,
        out_shape=outs,
        scratch_shapes=scratch,
        input_output_aliases=aliases,
        compiler_params=pltpu.CompilerParams(vmem_limit_bytes=VMEM_LIMIT),
        cost_estimate=pl.CostEstimate(flops=20_000_000_000, bytes_accessed=4_000_000, transcendentals=0),
        name=f"pivot_block_{k}",
    )(*args)


def cut_kernel(front, *outs):
    start = 0
    for out in outs:
        count = out.shape[0]
        out[...] = front[0, start : start + count, :]
        start += count


def cut(front, chunks):
    rows, width = front.shape[1], front.shape[2] - NPIV
    return pl.pallas_call(
        cut_kernel,
        grid=(width // PB,),
        in_specs=[pl.BlockSpec((1, rows, PB), lambda i: (0, 0, NPB + i))],
        out_specs=[pl.BlockSpec((c, PB), lambda i: (0, i)) for c in chunks],
        out_shape=[jax.ShapeDtypeStruct((c, width), jnp.float32) for c in chunks],
        compiler_params=pltpu.CompilerParams(vmem_limit_bytes=VMEM_LIMIT),
        name="cut_rows",
    )(front)


def transposed_base_kernel(w, own, *refs):
    chunks, (out_ref, own_ref) = refs[:-2], refs[-2:]

    @pl.when(pl.program_id(0) == 0)
    def _():
        own_ref[...] = own[...].T

    entries = jnp.concatenate([c[...] for c in chunks], axis=0)
    out_ref[...] = entries.T - dot_nn(w[...], own_ref[...])


def transposed_base(chunks, own, gathered):
    rows, depth = own.shape
    width = chunks[0].shape[1]
    return pl.pallas_call(
        transposed_base_kernel,
        grid=(width // PB,),
        in_specs=[pl.BlockSpec((PB, depth), lambda i: (NPB + i, 0)), whole(own.shape)]
        + [pl.BlockSpec((c.shape[0], PB), lambda i: (0, i)) for c in chunks],
        out_specs=pl.BlockSpec((PB, rows), lambda i: (i, 0)),
        out_shape=jax.ShapeDtypeStruct((width, rows), jnp.float32),
        scratch_shapes=[pltpu.VMEM((depth, rows), jnp.bfloat16)],
        compiler_params=pltpu.CompilerParams(vmem_limit_bytes=VMEM_LIMIT),
        name="transposed_base",
    )(gathered, own, *chunks)


def contribution_kernel(target_ref, info_ref, base, w, own, out_ref, own_ref):
    i = pl.program_id(0)
    rows = own.shape[0]

    @pl.when(i == 0)
    def _():
        own_ref[...] = own[...].T
        out_ref[...] = jnp.zeros_like(out_ref)

    ids = lax.broadcasted_iota(jnp.int32, (TILE, rows), 1) + info_ref[0]
    keep = (ids >= NPIV) & (ids < NPIV + info_ref[1] * TILE)
    value = base[...] - dot_nn(w[...], own_ref[...])
    count = value.shape[0] // TILE
    for n in range(count):

        @pl.when(count * i + n < info_ref[1])
        def _():
            target = target_ref[count * i + n]
            at = pl.multiple_of(target % 2 * TILE, TILE)
            tile = jnp.where(keep, value[n * TILE : (n + 1) * TILE], 0.0)
            out_ref[target // 2, pl.ds(at, TILE), :] = tile.astype(jnp.bfloat16)


def contributions(targets, info, base, own, gathered):
    width, rows = base.shape
    depth = own.shape[1]
    return pl.pallas_call(
        contribution_kernel,
        grid_spec=pltpu.PrefetchScalarGridSpec(
            num_scalar_prefetch=2,
            grid=(width // PB,),
            in_specs=[
                pl.BlockSpec((PB, rows), lambda i, target, info: (i, 0)),
                pl.BlockSpec((PB, depth), lambda i, target, info: (NPB + i, 0)),
                pl.BlockSpec((rows, depth), lambda i, target, info: (0, 0)),
            ],
            out_specs=pl.BlockSpec((PT // 2, 2 * TILE, rows), lambda i, target, info: (0, 0, 0)),
            scratch_shapes=[pltpu.VMEM((depth, rows), jnp.bfloat16)],
        ),
        out_shape=jax.ShapeDtypeStruct((PT // 2, 2 * TILE, rows), jnp.bfloat16),
        compiler_params=pltpu.CompilerParams(vmem_limit_bytes=VMEM_LIMIT),
        name="contributions",
    )(targets, info, base, gathered, own)


def place_kernel(source_ref, *refs):
    tiles, out_ref = refs[:-1], refs[-1]
    i = pl.program_id(0)
    for n, tile in enumerate(tiles):
        live = source_ref[len(tiles) * i + n] < CT
        out_ref[:, n * TILE : (n + 1) * TILE] = jnp.where(live, tile[0], jnp.zeros_like(tile[0]))


def place(sources, incoming, per_step=8):
    _, width, rows = incoming.shape
    skip = NPIV // rows
    each = rows // TILE

    def pick(n):
        def index(i, source):
            tile = jnp.minimum(source[per_step * i + n], CT - 1)
            return skip + tile // each, 0, tile % each

        return index

    return pl.pallas_call(
        place_kernel,
        grid_spec=pltpu.PrefetchScalarGridSpec(
            num_scalar_prefetch=1,
            grid=(PT // per_step,),
            in_specs=[pl.BlockSpec((1, width, TILE), pick(n)) for n in range(per_step)],
            out_specs=pl.BlockSpec((width, per_step * TILE), lambda i, source: (0, i)),
        ),
        out_shape=jax.ShapeDtypeStruct((width, PT * TILE), jnp.bfloat16),
        compiler_params=pltpu.CompilerParams(vmem_limit_bytes=VMEM_LIMIT),
        name="parent_rows",
    )(sources, *([incoming] * per_step))


def exchange(array):
    return lax.all_to_all(array, "helper", split_axis=0, concat_axis=0, tiled=True)


def local(front, tile_map, live_tiles):
    _, rows, order = front.shape
    helpers = lax.axis_size("helper")
    helper = lax.axis_index("helper")
    first_row = (helper * rows).astype(jnp.int32).reshape(1)
    piece = rows // helpers

    chunks = cut(front, CHUNKS)

    panel = front[0, :, :NPIV]
    scattered = exchange(panel.reshape(helpers, piece, NPIV))[: NPIV // rows]
    scattered, *chunks = lax.optimization_barrier((scattered, *chunks))
    block_0 = exchange(jnp.broadcast_to(scattered[None, :2, :, :PB], (helpers, 2, piece, PB)))
    rest = lax.all_gather(scattered[2:], "helper", axis=0)
    chunks[0] = shifted(chunks[0], "front", 1)

    tiling = shifted(jnp.concatenate([tile_map[0], live_tiles]), "front", 1)
    targets, live_count = tiling[:CT], tiling[CT]
    sources = tile_sources(targets, live_count)
    info = jnp.concatenate([first_row, live_count.reshape(1)])

    block_0, *chunks = lax.optimization_barrier((block_0, *chunks))
    inv0, diag0, factor, wb0 = factor_step(0, first_row, front, [(block_0, 0, 0)], [], None)
    chunks[1] = shifted(chunks[1], "front", 1)

    wb0, *chunks = lax.optimization_barrier((wb0, *chunks))
    own0 = shifted(wb0, "front", 1)
    inv0, own0, *chunks = lax.optimization_barrier((inv0, own0, *chunks))
    all0 = lax.all_gather(own0, "helper", axis=0, tiled=True)
    inv1, diag1, factor, wb1, lb10 = factor_step(
        1, first_row, front, [(rest, 0, 0), (rest, 0, 1)], [inv0, wb0], factor
    )
    chunks[2] = shifted(chunks[2], "front", 1)

    inv1, wb1, *chunks = lax.optimization_barrier((inv1, wb1, *chunks))
    diag2, factor, wb2 = factor_step(
        2, first_row, front, [(rest, 1, 0), (rest, 1, 1), (rest, 1, 2)], [inv0, inv1, lb10, wb0, wb1], factor
    )
    own1 = shifted(wb1, "front", 1)
    chunks[3] = shifted(chunks[3], "front", 1)

    wb2, own1, *chunks = lax.optimization_barrier((wb2, own1, *chunks))
    own2 = shifted(wb2, "front", 1)
    own2, *chunks = lax.optimization_barrier((own2, *chunks))
    own12 = jnp.concatenate([own1, own2], axis=1)
    all12 = lax.all_gather(own12, "helper", axis=0, tiled=True)
    chunks[4] = shifted(chunks[4], "front", 1)

    base = transposed_base(chunks, own0, all0)
    outgoing = contributions(targets, info, base, own12, all12)
    parent = place(sources, exchange(outgoing))
    diag = jnp.concatenate([diag0, diag1, diag2], axis=1)
    return factor[None], diag * diag, parent[None]


def tile_sources(mapping, live_count):
    tile_ids = lax.iota(jnp.int32, CT)[None, :]
    match = (mapping[None, :] == lax.iota(jnp.int32, PT)[:, None]) & (tile_ids < live_count)
    found = jnp.sum(jnp.where(match, tile_ids + 1, 0), axis=1)
    return jnp.where(found > 0, found - 1, CT).astype(jnp.int32)


def solution(mesh):
    placed = (P("front", "helper", None), P("front", None), P("front"))
    return jax.shard_map(
        local,
        mesh=mesh,
        in_specs=placed,
        out_specs=(P("front", "helper", None), P("front", None), P("front", "helper", None)),
        check_vma=False,
    )
```

```python
import functools

import jax
import jax.numpy as jnp
from jax import lax
from jax.experimental import pallas as pl
from jax.experimental.pallas import tpu as pltpu
from jax.sharding import PartitionSpec as P

PB = 512
NPB = 3
TILE = 128
NPIV = 1536
CT = 52
PT = 64
SKIP = NPIV // TILE
VMEM_LIMIT = 48 << 20
VMEM_MOST = 62 << 20
CHUNKS = (24, 32, 32, 80, 88)
HIGHEST = lax.Precision.HIGHEST


def shifted(array, axis, by):
    count = lax.axis_size(axis)
    return lax.ppermute(array, axis, [(i, (i + by) % count) for i in range(count)])


def dot_nt(a, b, precision=None):
    return lax.dot_general(
        a, b, (((1,), (1,)), ((), ())), precision=precision, preferred_element_type=jnp.float32
    )


def dot_nn(a, b, precision=None):
    return lax.dot_general(
        a, b, (((1,), (0,)), ((), ())), precision=precision, preferred_element_type=jnp.float32
    )


def leaf_inverse(strips, corner_ref):
    lanes = lax.broadcasted_iota(jnp.int32, (8, TILE), 1)
    subs = lax.broadcasted_iota(jnp.int32, (8, TILE), 0)
    count = len(strips)
    t = list(strips)
    e = [jnp.where(lanes == subs + 8 * r, 1.0, 0.0).astype(jnp.float32) for r in range(count)]
    diag = jnp.zeros((8, TILE), jnp.float32)

    def row_splat(v, i):
        return jnp.broadcast_to(v[i : i + 1, :], (8, TILE))

    def lane_splat(v, c):
        return jnp.broadcast_to(v[:, c : c + 1], (8, TILE))

    out = []
    for s in range(count):
        k = 8 * s
        last = s + 1 == count
        corner = [[None] * 8 for _ in range(8)]
        for j in range(8):
            slot = s % 2 * 8 + j
            corner_ref[slot] = lane_splat(t[s], k + j)
            for i in range(j, 8):
                corner[i][j] = row_splat(corner_ref[slot], i)
        rt = None if last else [row_splat(t[s], i) for i in range(8)]
        re = [row_splat(e[s], i) for i in range(8)]
        l = [[None] * 8 for _ in range(8)]
        inv = []
        for j in range(8):
            iv = lax.rsqrt(corner[j][j])
            inv.append(iv)
            diag = jnp.where(lanes == k + j, corner[j][j] * iv, diag)
            for i in range(j + 1, 8):
                l[i][j] = corner[i][j] * iv
            for i in range(j + 1, 8):
                for m in range(j + 1, i + 1):
                    corner[i][m] = corner[i][m] - l[i][j] * l[m][j]
            re[j] = re[j] * iv
            if not last:
                rt[j] = rt[j] * iv
            for i in range(j + 1, 8):
                re[i] = re[i] - l[i][j] * re[j]
                if not last:
                    rt[i] = rt[i] - l[i][j] * rt[j]
        rows = re[0]
        for i in range(1, 8):
            rows = jnp.where(subs == i, re[i], rows)
        out.append(rows)
        for r in range(s + 1, count):
            c = [lane_splat(t[r], k + j) for j in range(8)]
            for j in range(8):
                c[j] = c[j] * inv[j]
                for m in range(j + 1, 8):
                    c[m] = c[m] - c[j] * l[m][j]
                t[r] = t[r] - c[j] * rt[j]
                e[r] = e[r] - c[j] * re[j]
    return out, diag[0:1, :]


def block_inverse(ax_ref, diag_ref, leaf_ref, corner_ref):
    steps = PB // TILE
    ax_ref[:, PB : 2 * PB] = jnp.zeros((PB, PB), jnp.float32)

    def step(j, carry):
        o = pl.multiple_of(j * TILE, TILE)
        strips = [
            ax_ref[pl.ds(pl.multiple_of(o + 8 * r, 8), 8), pl.ds(o, TILE)] for r in range(TILE // 8)
        ]
        rows, diag = leaf_inverse(strips, corner_ref)
        for r in range(TILE // 8):
            leaf_ref[8 * r : 8 * r + 8, :] = rows[r]
        diag_ref[:, pl.ds(o, TILE)] = diag
        for q in range(steps):

            @pl.when(j == q)
            def _():
                lo, hi = q * TILE, (q + 1) * TILE
                leaf = leaf_ref[...]
                row = dot_nn(leaf, ax_ref[lo:hi, hi : PB + lo], HIGHEST)
                ax_ref[lo:hi, hi : PB + lo] = row
                ax_ref[lo:hi, PB + lo : PB + hi] = leaf
                if q + 1 < steps:
                    column = dot_nt(ax_ref[hi:PB, lo:hi], leaf, HIGHEST)
                    row = jnp.concatenate([row, leaf], axis=1)
                    ax_ref[hi:PB, hi : PB + hi] -= dot_nn(column, row, HIGHEST)

        return carry

    lax.fori_loop(0, steps, step, 0)


def finish_panel(k, first_row, panel, inv, diag):
    w = dot_nt(panel, inv, HIGHEST)
    rows = lax.broadcasted_iota(jnp.int32, w.shape, 0) + first_row
    w = jnp.where(rows >= k * PB, w, 0.0)
    return w.astype(jnp.bfloat16), w * (1.0 / diag)


def put_block(ref):
    return jnp.concatenate([ref[:, s].reshape(256, PB) for s in range(2)], axis=0)


def kernel_0(row_ref, a00, panel, inv_ref, diag_ref, factor_ref, wb_ref, ax_ref, leaf_ref, corner_ref):
    ax_ref[:, 0:PB] = put_block(a00)
    block_inverse(ax_ref, diag_ref, leaf_ref, corner_ref)
    inv = ax_ref[:, PB : 2 * PB]
    inv_ref[...] = inv
    wb_ref[...], factor_ref[...] = finish_panel(0, row_ref[0], panel[0], inv, diag_ref[...])


def kernel_12(
    row_ref, a02, a10, a11, a21, a22, p1, p2, inv0, wb0, diag1_ref, diag2_ref, factor_ref, wb_ref, ax_ref, leaf_ref,
    corner_ref, lb20_ref, lb21_ref, a21_ref, a22_ref, p2_ref
):
    lb10 = dot_nt(put_block(a10), inv0[...], HIGHEST).astype(jnp.bfloat16)
    lb20_ref[...] = dot_nn(inv0[...], put_block(a02), HIGHEST).T.astype(jnp.bfloat16)
    ax_ref[:, 0:PB] = put_block(a11) - dot_nt(lb10, lb10)
    a21_ref[...] = put_block(a21) - dot_nt(lb20_ref[...], lb10)
    a22_ref[...] = put_block(a22) - dot_nt(lb20_ref[...], lb20_ref[...])
    mine = p1[0] - dot_nt(wb0[...], lb10)
    p2_ref[...] = p2[0] - dot_nt(wb0[...], lb20_ref[...])
    block_inverse(ax_ref, diag1_ref, leaf_ref, corner_ref)
    inv = ax_ref[:, PB : 2 * PB]
    lb21 = dot_nt(a21_ref[...], inv, HIGHEST).astype(jnp.bfloat16)
    lb21_ref[...] = lb21
    wb, factor = finish_panel(1, row_ref[0], mine, inv, diag1_ref[...])
    wb_ref[:, 0:PB], factor_ref[:, 0:PB] = wb, factor
    ax_ref[:, 0:PB] = a22_ref[...] - dot_nt(lb21, lb21)
    block_inverse(ax_ref, diag2_ref, leaf_ref, corner_ref)
    mine = p2_ref[...] - dot_nt(wb_ref[:, 0:PB], lb21_ref[...])
    wb, factor = finish_panel(2, row_ref[0], mine, ax_ref[:, PB : 2 * PB], diag2_ref[...])
    wb_ref[:, PB : 2 * PB], factor_ref[:, PB : 2 * PB] = wb, factor


def whole(shape):
    return pl.BlockSpec(shape, lambda i: (0,) * len(shape))


def factor_step(blocks, first_row, args, specs, rows):
    first = blocks[0] == 0
    width = len(blocks) * PB
    outs = [jax.ShapeDtypeStruct((1, PB), jnp.float32) for _ in blocks]
    outs += [jax.ShapeDtypeStruct((rows, width), jnp.float32), jax.ShapeDtypeStruct((rows, width), jnp.bfloat16)]
    square = jax.ShapeDtypeStruct((PB, PB), jnp.float32)
    scratch = [pltpu.VMEM((PB, 2 * PB), jnp.float32), pltpu.VMEM((TILE, TILE), jnp.float32)]
    scratch.append(pltpu.VMEM((16, 8, TILE), jnp.float32))
    if first:
        outs.insert(0, square)
    else:
        scratch += [pltpu.VMEM((PB, PB), jnp.bfloat16)] * 2 + [pltpu.VMEM((PB, PB), jnp.float32)] * 2
        scratch.append(pltpu.VMEM((rows, PB), jnp.float32))
    return pl.pallas_call(
        kernel_0 if first else kernel_12,
        grid=(1,),
        in_specs=[pl.BlockSpec(memory_space=pltpu.SMEM), *specs],
        out_specs=[whole(x.shape) for x in outs],
        out_shape=outs,
        scratch_shapes=scratch,
        compiler_params=pltpu.CompilerParams(vmem_limit_bytes=VMEM_LIMIT if first else VMEM_MOST),
        cost_estimate=pl.CostEstimate(flops=20_000_000_000 * len(blocks), bytes_accessed=4_000_000, transcendentals=0),
        name=f"pivot_block_{blocks[0]}",
    )(first_row, *args)


def cut_kernel(front, *outs):
    start = 0
    for out in outs:
        count = out.shape[0]
        out[...] = front[0, start : start + count, :]
        start += count


def cut(front, chunks):
    rows, width = front.shape[1], front.shape[2] - NPIV
    return pl.pallas_call(
        cut_kernel,
        grid=(width // PB,),
        in_specs=[pl.BlockSpec((1, rows, PB), lambda i: (0, 0, NPB + i))],
        out_specs=[pl.BlockSpec((c, PB), lambda i: (0, i)) for c in chunks],
        out_shape=[pltpu.HBM((c, width), jnp.float32) for c in chunks],
        compiler_params=pltpu.CompilerParams(vmem_limit_bytes=VMEM_LIMIT),
        name="cut_rows",
    )(front)


def transposed_base_kernel(w, own, *refs):
    chunks, (out_ref, own_ref) = refs[:-2], refs[-2:]

    @pl.when(pl.program_id(0) == 0)
    def _():
        own_ref[...] = own[...].T

    entries = jnp.concatenate([c[...] for c in chunks], axis=0)
    out_ref[...] = entries.T - dot_nn(w[...], own_ref[...])


def transposed_base(chunks, own, gathered):
    rows, depth = own.shape
    width = chunks[0].shape[1]
    return pl.pallas_call(
        transposed_base_kernel,
        grid=(width // PB,),
        in_specs=[pl.BlockSpec((PB, depth), lambda i: (NPB + i, 0)), whole(own.shape)]
        + [pl.BlockSpec((c.shape[0], PB), lambda i: (0, i)) for c in chunks],
        out_specs=pl.BlockSpec((PB, rows), lambda i: (i, 0)),
        out_shape=jax.ShapeDtypeStruct((width, rows), jnp.float32),
        scratch_shapes=[pltpu.VMEM((depth, rows), jnp.bfloat16)],
        compiler_params=pltpu.CompilerParams(vmem_limit_bytes=VMEM_LIMIT),
        name="transposed_base",
    )(gathered, own, *chunks)


def contribution_kernel(target_ref, info_ref, base, w, own, out_ref, own_ref):
    i = pl.program_id(0)
    rows = own.shape[0]

    @pl.when(i == 0)
    def _():
        own_ref[...] = own[...].T
        out_ref[...] = jnp.zeros_like(out_ref)

    ids = lax.broadcasted_iota(jnp.int32, (TILE, rows), 1) + info_ref[0]
    keep = (ids >= NPIV) & (ids < NPIV + info_ref[1] * TILE)
    value = base[...] - dot_nn(w[...], own_ref[...])
    count = value.shape[0] // TILE
    for n in range(count):
        target = target_ref[count * i + n]
        live = count * i + n < info_ref[1]
        at = pl.multiple_of(target % 2 * TILE, TILE)
        tile = jnp.where(keep & live, value[n * TILE : (n + 1) * TILE], 0.0)
        out_ref[target // 2, pl.ds(at, TILE), :] = tile.astype(jnp.bfloat16)


def contributions(targets, info, base, own, gathered):
    width, rows = base.shape
    depth = own.shape[1]
    return pl.pallas_call(
        contribution_kernel,
        grid_spec=pltpu.PrefetchScalarGridSpec(
            num_scalar_prefetch=2,
            grid=(width // PB,),
            in_specs=[
                pl.BlockSpec((PB, rows), lambda i, target, info: (i, 0)),
                pl.BlockSpec((PB, depth), lambda i, target, info: (NPB + i, 0)),
                pl.BlockSpec((rows, depth), lambda i, target, info: (0, 0)),
            ],
            out_specs=pl.BlockSpec((PT // 2, 2 * TILE, rows), lambda i, target, info: (0, 0, 0)),
            scratch_shapes=[pltpu.VMEM((depth, rows), jnp.bfloat16)],
        ),
        out_shape=pltpu.HBM((PT // 2, 2 * TILE, rows), jnp.bfloat16),
        compiler_params=pltpu.CompilerParams(vmem_limit_bytes=VMEM_LIMIT),
        name="contributions",
    )(targets, info, base, gathered, own)


def place_kernel(source_ref, *refs):
    tiles, out_ref = refs[:-1], refs[-1]
    i = pl.program_id(0)
    for n, tile in enumerate(tiles):
        live = source_ref[len(tiles) * i + n] < CT
        out_ref[:, n * TILE : (n + 1) * TILE] = jnp.where(live, tile[0], jnp.zeros_like(tile[0]))


def place(sources, incoming, per_step=8):
    _, width, rows = incoming.shape
    skip = NPIV // rows
    each = rows // TILE

    def pick(n):
        def index(i, source):
            tile = jnp.minimum(source[per_step * i + n], CT - 1)
            return skip + tile // each, 0, tile % each

        return index

    return pl.pallas_call(
        place_kernel,
        grid_spec=pltpu.PrefetchScalarGridSpec(
            num_scalar_prefetch=1,
            grid=(PT // per_step,),
            in_specs=[pl.BlockSpec((1, width, TILE), pick(n)) for n in range(per_step)],
            out_specs=pl.BlockSpec((width, per_step * TILE), lambda i, source: (0, i)),
        ),
        out_shape=jax.ShapeDtypeStruct((width, PT * TILE), jnp.bfloat16),
        compiler_params=pltpu.CompilerParams(vmem_limit_bytes=VMEM_LIMIT),
        name="parent_rows",
    )(sources, *([incoming] * per_step))


def exchange(array):
    return lax.all_to_all(array, "helper", split_axis=0, concat_axis=0, tiled=True)


def local(front, tile_map, live_tiles):
    _, rows, order = front.shape
    helpers = lax.axis_size("helper")
    helper = lax.axis_index("helper")
    first_row = (helper * rows).astype(jnp.int32).reshape(1)
    piece = rows // helpers

    chunks = list(cut(front, CHUNKS))

    pair = helper // (PB // rows)
    first = jnp.where(pair == 2, 1, 0) * PB
    second = jnp.where(pair == 1, 1, 2) * PB
    panel = jnp.concatenate([lax.dynamic_slice(front[0], (0, c), (rows, PB)) for c in (first, second)], axis=1)
    scattered = exchange(panel.reshape(helpers, piece, 2 * PB))[: NPIV // rows]
    scattered, *chunks = lax.optimization_barrier((scattered, *chunks))
    block_0 = exchange(jnp.broadcast_to(scattered[None, :2, :, :PB], (helpers, 2, piece, PB)))
    rest = lax.all_gather(scattered, "helper", axis=0)
    chunks[0] = shifted(chunks[0], "front", 1)

    tiling = shifted(jnp.concatenate([tile_map[0], live_tiles]), "front", 1)
    targets, live_count = tiling[:CT], tiling[CT]
    sources = tile_sources(targets, live_count)
    info = jnp.concatenate([first_row, live_count.reshape(1)])

    block_0, *chunks = lax.optimization_barrier((block_0, *chunks))
    panel_0 = pl.BlockSpec((1, rows, PB), lambda _: (0, 0, 0))
    specs = [whole(block_0.shape), panel_0]
    inv0, diag0, factor0, wb0 = factor_step((0,), first_row, [block_0, front], specs, rows)
    chunks[1] = shifted(chunks[1], "front", 1)
    chunks[2] = shifted(chunks[2], "front", -1)

    wb0, *chunks = lax.optimization_barrier((wb0, *chunks))
    own0 = shifted(wb0, "front", 1)
    inv0, own0, *chunks = lax.optimization_barrier((inv0, own0, *chunks))
    all0 = lax.all_gather(own0, "helper", axis=0, tiled=True)
    specs = [
        pl.BlockSpec((helpers, 2, piece, PB), lambda _, i=i, j=j: (0, i, 0, j))
        for i, j in [(0, 1), (1, 0), (1, 1), (2, 0), (2, 1)]
    ]
    specs += [pl.BlockSpec((1, rows, PB), lambda _, k=k: (0, 0, k)) for k in (1, 2)]
    specs += [whole(inv0.shape), whole(wb0.shape)]
    args = [rest] * 5 + [front] * 2 + [inv0, wb0]
    diag1, diag2, factor12, wb12 = factor_step((1, 2), first_row, args, specs, rows)
    chunks[3] = shifted(chunks[3], "front", 1)
    chunks[2] = shifted(chunks[2], "front", -1)

    wb12, *chunks = lax.optimization_barrier((wb12, *chunks))
    own12 = shifted(wb12, "front", 1)
    own12, *chunks = lax.optimization_barrier((own12, *chunks))
    all12 = lax.all_gather(own12, "helper", axis=0, tiled=True)
    chunks[2] = shifted(chunks[2], "front", -1)
    chunks[4] = shifted(chunks[4], "front", 1)

    base = transposed_base(chunks, own0, all0)
    outgoing = contributions(targets, info, base, own12, all12)
    parent = place(sources, exchange(outgoing))
    diag = jnp.concatenate([diag0, diag1, diag2], axis=1)
    factor = jnp.concatenate([factor0, factor12], axis=1)
    return factor[None], diag * diag, parent[None]


def tile_sources(mapping, live_count):
    tile_ids = lax.iota(jnp.int32, CT)[None, :]
    match = (mapping[None, :] == lax.iota(jnp.int32, PT)[:, None]) & (tile_ids < live_count)
    found = jnp.sum(jnp.where(match, tile_ids + 1, 0), axis=1)
    return jnp.where(found > 0, found - 1, CT).astype(jnp.int32)


def solution(mesh):
    placed = (P("front", "helper", None), P("front", None), P("front"))
    return jax.shard_map(
        local,
        mesh=mesh,
        in_specs=placed,
        out_specs=(P("front", "helper", None), P("front", None), P("front", "helper", None)),
        check_vma=False,
    )
```

```python
import functools

import jax
import jax.numpy as jnp
from jax import lax
from jax.experimental import pallas as pl
from jax.experimental.pallas import tpu as pltpu
from jax.sharding import PartitionSpec as P

PB = 512
NPB = 3
TILE = 128
NPIV = 1536
CT = 52
PT = 64
SKIP = NPIV // TILE
VMEM_LIMIT = 48 << 20
VMEM_MOST = 62 << 20
WIDE = 13 * TILE
CHUNKS = (24, 32, 32, 80, 88)
HIGHEST = lax.Precision.HIGHEST


def shifted(array, axis, by):
    count = lax.axis_size(axis)
    return lax.ppermute(array, axis, [(i, (i + by) % count) for i in range(count)])


def dot_nt(a, b, precision=None):
    return lax.dot_general(
        a, b, (((1,), (1,)), ((), ())), precision=precision, preferred_element_type=jnp.float32
    )


def dot_nn(a, b, precision=None):
    return lax.dot_general(
        a, b, (((1,), (0,)), ((), ())), precision=precision, preferred_element_type=jnp.float32
    )


def leaf_inverse(strips, corner_ref):
    lanes = lax.broadcasted_iota(jnp.int32, (8, TILE), 1)
    subs = lax.broadcasted_iota(jnp.int32, (8, TILE), 0)
    count = len(strips)
    t = list(strips)
    e = [jnp.where(lanes == subs + 8 * r, 1.0, 0.0).astype(jnp.float32) for r in range(count)]
    diag = jnp.zeros((8, TILE), jnp.float32)

    def row_splat(v, i):
        return jnp.broadcast_to(v[i : i + 1, :], (8, TILE))

    def lane_splat(v, c):
        return jnp.broadcast_to(v[:, c : c + 1], (8, TILE))

    out = []
    for s in range(count):
        k = 8 * s
        last = s + 1 == count
        corner = [[None] * 8 for _ in range(8)]
        if s == 0:
            b = [lane_splat(t[0], j) for j in range(8)]
        for j in range(8):
            slot = s % 2 * 8 + j
            corner_ref[slot] = b[j]
            for i in range(j, 8):
                corner[i][j] = row_splat(corner_ref[slot], i)
        rt = None if last else [row_splat(t[s], i) for i in range(8)]
        re = [row_splat(e[s], i) for i in range(8)]
        l = [[None] * 8 for _ in range(8)]
        inv = []
        for j in range(8):
            iv = lax.rsqrt(corner[j][j])
            inv.append(iv)
            diag = jnp.where(lanes == k + j, corner[j][j] * iv, diag)
            for i in range(j + 1, 8):
                l[i][j] = corner[i][j] * iv
            for i in range(j + 1, 8):
                for m in range(j + 1, i + 1):
                    corner[i][m] = corner[i][m] - l[i][j] * l[m][j]
            re[j] = re[j] * iv
            if not last:
                rt[j] = rt[j] * iv
            for i in range(j + 1, 8):
                re[i] = re[i] - l[i][j] * re[j]
                if not last:
                    rt[i] = rt[i] - l[i][j] * rt[j]
        rows = re[0]
        for i in range(1, 8):
            rows = jnp.where(subs == i, re[i], rows)
        out.append(rows)
        for r in range(s + 1, count):
            c = [lane_splat(t[r], k + j) for j in range(8)]
            if r == s + 1:
                b = [lane_splat(t[r], k + 8 + j) for j in range(8)]
            for j in range(8):
                c[j] = c[j] * inv[j]
                if r == s + 1:
                    slot = 16 + s % 2 * 8 + j
                    corner_ref[slot] = c[j]
                    for m in range(8):
                        b[m] = b[m] - c[j] * row_splat(corner_ref[slot], m)
                for m in range(j + 1, 8):
                    c[m] = c[m] - c[j] * l[m][j]
                t[r] = t[r] - c[j] * rt[j]
                e[r] = e[r] - c[j] * re[j]
    return out, diag[0:1, :]


def block_inverse(ax_ref, diag_ref, leaf_ref, corner_ref):
    steps = PB // TILE
    ax_ref[:, PB : 2 * PB] = jnp.zeros((PB, PB), jnp.float32)

    def step(j, carry):
        o = pl.multiple_of(j * TILE, TILE)
        strips = [
            ax_ref[pl.ds(pl.multiple_of(o + 8 * r, 8), 8), pl.ds(o, TILE)] for r in range(TILE // 8)
        ]
        rows, diag = leaf_inverse(strips, corner_ref)
        for r in range(TILE // 8):
            leaf_ref[8 * r : 8 * r + 8, :] = rows[r]
        diag_ref[:, pl.ds(o, TILE)] = diag
        for q in range(steps):

            @pl.when(j == q)
            def _():
                lo, hi = q * TILE, (q + 1) * TILE
                leaf = leaf_ref[...]
                row = dot_nn(leaf, ax_ref[lo:hi, hi : PB + lo], HIGHEST)
                ax_ref[lo:hi, hi : PB + lo] = row
                ax_ref[lo:hi, PB + lo : PB + hi] = leaf
                if q + 1 < steps:
                    column = dot_nt(ax_ref[hi:PB, lo:hi], leaf, HIGHEST)
                    row = jnp.concatenate([row, leaf], axis=1)
                    ax_ref[hi:PB, hi : PB + hi] -= dot_nn(column, row, HIGHEST)

        return carry

    lax.fori_loop(0, steps, step, 0)


def finish_panel(k, first_row, panel, inv, diag):
    w = dot_nt(panel, inv, HIGHEST)
    rows = lax.broadcasted_iota(jnp.int32, w.shape, 0) + first_row
    w = jnp.where(rows >= k * PB, w, 0.0)
    return w.astype(jnp.bfloat16), w * (1.0 / diag)


def put_block(ref):
    return jnp.concatenate([ref[:, s].reshape(256, PB) for s in range(2)], axis=0)


def kernel_0(row_ref, a00, panel, inv_ref, diag_ref, factor_ref, wb_ref, ax_ref, leaf_ref, corner_ref):
    ax_ref[:, 0:PB] = put_block(a00)
    block_inverse(ax_ref, diag_ref, leaf_ref, corner_ref)
    inv = ax_ref[:, PB : 2 * PB]
    inv_ref[...] = inv
    wb_ref[...], factor_ref[...] = finish_panel(0, row_ref[0], panel[0], inv, diag_ref[...])


def kernel_12(
    row_ref, a10, a11, inv0, wb0, rest, front, diag1_ref, diag2_ref, factor_ref, wb_ref, ax_ref, leaf_ref, corner_ref,
    lb10_ref, lb20_ref, lb21_ref, a21_ref, p2_ref, a02, a21, a22, p1, p2, sems
):
    copies = [
        pltpu.make_async_copy(source, target, sems.at[n])
        for n, (source, target) in enumerate(
            (
                (rest.at[:, 0:2, :, PB : 2 * PB], a02),
                (rest.at[:, 4:6, :, 0:PB], a21),
                (rest.at[:, 4:6, :, PB : 2 * PB], a22),
                (front.at[0, :, PB : 2 * PB], p1),
                (front.at[0, :, 2 * PB : 3 * PB], p2),
            )
        )
    ]
    for copy in copies:
        copy.start()
    lb10_ref[...] = dot_nt(put_block(a10), inv0[...], HIGHEST).astype(jnp.bfloat16)
    ax_ref[:, 0:PB] = put_block(a11) - dot_nt(lb10_ref[...], lb10_ref[...])
    block_inverse(ax_ref, diag1_ref, leaf_ref, corner_ref)
    for copy in copies:
        copy.wait()
    inv = ax_ref[:, PB : 2 * PB]
    lb10 = lb10_ref[...]
    lb20 = dot_nn(inv0[...], put_block(a02), HIGHEST).T.astype(jnp.bfloat16)
    lb20_ref[...] = lb20
    a21_ref[...] = put_block(a21) - dot_nt(lb20, lb10)
    lb21 = dot_nt(a21_ref[...], inv, HIGHEST).astype(jnp.bfloat16)
    lb21_ref[...] = lb21
    mine = p1[...] - dot_nt(wb0[...], lb10)
    wb, factor = finish_panel(1, row_ref[0], mine, inv, diag1_ref[...])
    wb_ref[:, 0:PB], factor_ref[:, 0:PB] = wb, factor
    p2_ref[...] = p2[...] - dot_nt(wb0[...], lb20_ref[...])
    ax_ref[:, 0:PB] = put_block(a22) - dot_nt(lb20_ref[...], lb20_ref[...]) - dot_nt(lb21, lb21)
    block_inverse(ax_ref, diag2_ref, leaf_ref, corner_ref)
    mine = p2_ref[...] - dot_nt(wb_ref[:, 0:PB], lb21_ref[...])
    wb, factor = finish_panel(2, row_ref[0], mine, ax_ref[:, PB : 2 * PB], diag2_ref[...])
    wb_ref[:, PB : 2 * PB], factor_ref[:, PB : 2 * PB] = wb, factor


def whole(shape):
    return pl.BlockSpec(shape, lambda i: (0,) * len(shape))


def factor_step(blocks, first_row, args, specs, rows):
    first = blocks[0] == 0
    width = len(blocks) * PB
    outs = [jax.ShapeDtypeStruct((1, PB), jnp.float32) for _ in blocks]
    outs += [jax.ShapeDtypeStruct((rows, width), jnp.float32), jax.ShapeDtypeStruct((rows, width), jnp.bfloat16)]
    square = jax.ShapeDtypeStruct((PB, PB), jnp.float32)
    scratch = [pltpu.VMEM((PB, 2 * PB), jnp.float32), pltpu.VMEM((TILE, TILE), jnp.float32)]
    scratch.append(pltpu.VMEM((32, 8, TILE), jnp.float32))
    if first:
        outs.insert(0, square)
    else:
        scratch += [pltpu.VMEM((PB, PB), jnp.bfloat16)] * 3
        scratch += [pltpu.VMEM((PB, PB), jnp.float32), pltpu.VMEM((rows, PB), jnp.float32)]
        scratch += [pltpu.VMEM((PB // 16, 2, 8, PB), jnp.float32)] * 3
        scratch += [pltpu.VMEM((rows, PB), jnp.float32)] * 2 + [pltpu.SemaphoreType.DMA((5,))]
    return pl.pallas_call(
        kernel_0 if first else kernel_12,
        grid=(1,),
        in_specs=[pl.BlockSpec(memory_space=pltpu.SMEM), *specs],
        out_specs=[whole(x.shape) for x in outs],
        out_shape=outs,
        scratch_shapes=scratch,
        compiler_params=pltpu.CompilerParams(vmem_limit_bytes=VMEM_LIMIT if first else VMEM_MOST),
        cost_estimate=pl.CostEstimate(flops=20_000_000_000 * len(blocks), bytes_accessed=4_000_000, transcendentals=0),
        name=f"pivot_block_{blocks[0]}",
    )(first_row, *args)


def cut_kernel(front, *outs):
    start = 0
    for out in outs:
        count = out.shape[0]
        out[...] = front[0, start : start + count, :]
        start += count


def cut(front, chunks):
    rows, width = front.shape[1], front.shape[2] - NPIV
    return pl.pallas_call(
        cut_kernel,
        grid=(width // PB,),
        in_specs=[pl.BlockSpec((1, rows, PB), lambda i: (0, 0, NPB + i))],
        out_specs=[pl.BlockSpec((c, PB), lambda i: (0, i)) for c in chunks],
        out_shape=[pltpu.HBM((c, width), jnp.float32) for c in chunks],
        compiler_params=pltpu.CompilerParams(vmem_limit_bytes=VMEM_LIMIT),
        name="cut_rows",
    )(front)


def transposed_base_kernel(w, own, *refs):
    chunks, (out_ref, own_ref) = refs[:-2], refs[-2:]

    @pl.when(pl.program_id(0) == 0)
    def _():
        own_ref[...] = own[...].T

    entries = jnp.concatenate([c[...] for c in chunks], axis=0)
    out_ref[...] = entries.T - dot_nn(w[...], own_ref[...])


def transposed_base(chunks, own, gathered):
    rows, depth = own.shape
    width = chunks[0].shape[1]
    return pl.pallas_call(
        transposed_base_kernel,
        grid=(width // PB,),
        in_specs=[pl.BlockSpec((PB, depth), lambda i: (NPB + i, 0)), whole(own.shape)]
        + [pl.BlockSpec((c.shape[0], PB), lambda i: (0, i)) for c in chunks],
        out_specs=pl.BlockSpec((PB, rows), lambda i: (i, 0)),
        out_shape=pltpu.HBM((width, rows), jnp.float32),
        scratch_shapes=[pltpu.VMEM((depth, rows), jnp.bfloat16)],
        compiler_params=pltpu.CompilerParams(vmem_limit_bytes=VMEM_LIMIT),
        name="transposed_base",
    )(gathered, own, *chunks)


def contribution_kernel(target_ref, info_ref, base, w, own, out_ref, own_ref):
    i = pl.program_id(0)
    rows = own.shape[0]

    @pl.when(i == 0)
    def _():
        own_ref[...] = own[...].T
        out_ref[...] = jnp.zeros_like(out_ref)

    ids = lax.broadcasted_iota(jnp.int32, (TILE, rows), 1) + info_ref[0]
    keep = (ids >= NPIV) & (ids < NPIV + info_ref[1] * TILE)
    value = base[...] - dot_nn(w[...], own_ref[...])
    count = value.shape[0] // TILE
    for n in range(count):
        target = target_ref[count * i + n]
        live = count * i + n < info_ref[1]
        at = pl.multiple_of(target % 2 * TILE, TILE)
        tile = jnp.where(keep & live, value[n * TILE : (n + 1) * TILE], 0.0)
        out_ref[target // 2, pl.ds(at, TILE), :] = tile.astype(jnp.bfloat16)


def contributions(targets, info, base, own, gathered):
    width, rows = base.shape
    depth = own.shape[1]
    return pl.pallas_call(
        contribution_kernel,
        grid_spec=pltpu.PrefetchScalarGridSpec(
            num_scalar_prefetch=2,
            grid=(width // WIDE,),
            in_specs=[
                pl.BlockSpec((WIDE, rows), lambda i, target, info: (i, 0)),
                pl.BlockSpec(
                    (pl.Element(WIDE), pl.Element(depth)), lambda i, target, info: (TILE * (SKIP + i * (WIDE // TILE)), 0)
                ),
                pl.BlockSpec((rows, depth), lambda i, target, info: (0, 0)),
            ],
            out_specs=pl.BlockSpec((PT // 2, 2 * TILE, rows), lambda i, target, info: (0, 0, 0)),
            scratch_shapes=[pltpu.VMEM((depth, rows), jnp.bfloat16)],
        ),
        out_shape=pltpu.HBM((PT // 2, 2 * TILE, rows), jnp.bfloat16),
        compiler_params=pltpu.CompilerParams(vmem_limit_bytes=VMEM_LIMIT),
        name="contributions",
    )(targets, info, base, gathered, own)


def place_kernel(source_ref, *refs):
    tiles, out_ref = refs[:-1], refs[-1]
    i = pl.program_id(0)
    for n, tile in enumerate(tiles):
        live = source_ref[len(tiles) * i + n] < CT
        out_ref[:, n * TILE : (n + 1) * TILE] = jnp.where(live, tile[0], jnp.zeros_like(tile[0]))


def place(sources, incoming, per_step=8):
    _, width, rows = incoming.shape
    skip = NPIV // rows
    each = rows // TILE

    def pick(n):
        def index(i, source):
            tile = jnp.minimum(source[per_step * i + n], CT - 1)
            return skip + tile // each, 0, tile % each

        return index

    return pl.pallas_call(
        place_kernel,
        grid_spec=pltpu.PrefetchScalarGridSpec(
            num_scalar_prefetch=1,
            grid=(PT // per_step,),
            in_specs=[pl.BlockSpec((1, width, TILE), pick(n)) for n in range(per_step)],
            out_specs=pl.BlockSpec((width, per_step * TILE), lambda i, source: (0, i)),
        ),
        out_shape=jax.ShapeDtypeStruct((width, PT * TILE), jnp.bfloat16),
        compiler_params=pltpu.CompilerParams(vmem_limit_bytes=VMEM_LIMIT),
        name="parent_rows",
    )(sources, *([incoming] * per_step))


def exchange(array):
    return lax.all_to_all(array, "helper", split_axis=0, concat_axis=0, tiled=True)


def local(front, tile_map, live_tiles):
    _, rows, order = front.shape
    helpers = lax.axis_size("helper")
    helper = lax.axis_index("helper")
    first_row = (helper * rows).astype(jnp.int32).reshape(1)
    piece = rows // helpers

    chunks = list(cut(front, CHUNKS))

    pair = helper // (PB // rows)
    first = jnp.where(pair == 2, 1, 0) * PB
    second = jnp.where(pair == 1, 1, 2) * PB
    panel = jnp.concatenate([lax.dynamic_slice(front[0], (0, c), (rows, PB)) for c in (first, second)], axis=1)
    scattered = exchange(panel.reshape(helpers, piece, 2 * PB))
    scattered, *chunks = lax.optimization_barrier((scattered, *chunks))
    block_0 = exchange(jnp.broadcast_to(scattered[None, :2, :, :PB], (helpers, 2, piece, PB)))
    rest = lax.all_gather(scattered[: NPIV // rows], "helper", axis=0)
    chunks[0] = shifted(chunks[0], "front", 1)

    tiling = shifted(jnp.concatenate([tile_map[0], live_tiles]), "front", 1)
    targets, live_count = tiling[:CT], tiling[CT]
    sources = tile_sources(targets, live_count)
    info = jnp.concatenate([first_row, live_count.reshape(1)])

    block_0, *chunks = lax.optimization_barrier((block_0, *chunks))
    panel_0 = pl.BlockSpec((1, rows, PB), lambda _: (0, 0, 0))
    specs = [whole(block_0.shape), panel_0]
    inv0, diag0, factor0, wb0 = factor_step((0,), first_row, [block_0, front], specs, rows)
    chunks[1] = shifted(chunks[1], "front", 1)
    chunks[2] = shifted(chunks[2], "front", -1)

    own0 = shifted(wb0, "front", 1)
    inv0, own0, *chunks = lax.optimization_barrier((inv0, own0, *chunks))
    all0 = lax.all_gather(own0, "helper", axis=0, tiled=True)
    specs = [pl.BlockSpec((helpers, 2, piece, PB), lambda _, j=j: (0, 1, 0, j)) for j in (0, 1)]
    specs += [whole(inv0.shape), whole(wb0.shape)] + [pl.BlockSpec(memory_space=pl.ANY)] * 2
    args = [rest, rest, inv0, wb0, rest, front]
    diag1, diag2, factor12, wb12 = factor_step((1, 2), first_row, args, specs, rows)
    chunks[3] = shifted(chunks[3], "front", 1)
    chunks[2] = shifted(chunks[2], "front", -1)

    wb12, *chunks = lax.optimization_barrier((wb12, *chunks))
    own12 = shifted(wb12, "front", 1)
    own12, *chunks = lax.optimization_barrier((own12, *chunks))
    all12 = lax.all_gather(own12, "helper", axis=0, tiled=True)
    chunks[2] = shifted(chunks[2], "front", -1)
    chunks[4] = shifted(chunks[4], "front", 1)

    base = transposed_base(chunks, own0, all0)
    outgoing = contributions(targets, info, base, own12, all12)
    parent = place(sources, exchange(outgoing))
    diag = jnp.concatenate([diag0, diag1, diag2], axis=1)
    factor = jnp.concatenate([factor0, factor12], axis=1)
    return factor[None], diag * diag, parent[None]


def tile_sources(mapping, live_count):
    tile_ids = lax.iota(jnp.int32, CT)[None, :]
    match = (mapping[None, :] == lax.iota(jnp.int32, PT)[:, None]) & (tile_ids < live_count)
    found = jnp.sum(jnp.where(match, tile_ids + 1, 0), axis=1)
    return jnp.where(found > 0, found - 1, CT).astype(jnp.int32)


def solution(mesh):
    placed = (P("front", "helper", None), P("front", None), P("front"))
    return jax.shard_map(
        local,
        mesh=mesh,
        in_specs=placed,
        out_specs=(P("front", "helper", None), P("front", None), P("front", "helper", None)),
        check_vma=False,
    )
```
